256 devices in a mesh: hst: 64 (over z, x, core), chip: 4 (over y).
Axes of the slice: x: 4, y: 4, z: 8, core: 2. Of those that a mesh axis runs over, the one named last changes fastest.
Arguments:
- data: bfloat16 [262144, 4096], P(('hst', 'chip')), as said below
- sketch: bfloat16 [4096, 128], replicated, may hold values from -0.09375 to 0.09375
Outputs:
- first_basis: float32 [262144, 128], P(('hst', 'chip'))
- basis: float32 [262144, 128], P(('hst', 'chip'))
- projected: float32 [128, 4096], replicated
The draws below stay inside these ranges and needn't reach their ends.
Inputs may be any that keep to these rules, and one draw needn't show every extreme that they name: `data`: rows and columns have unequal scales; the matrix has full column rank.
All inputs are finite; a program needn't handle non-finite values.
Results may differ from the reference program's by a relative error of at most 0.0029.
Values sent between devices are 32-bit elements; how exact they have to be, the bound alone decides.
No kernel may reach another device: no remote copies, remote signals or barrier semaphores. Data moves between devices by JAX's collectives and lax.ppermute only.
A program may use at most 128 MiB of HBM per device.

```python
import jax
import jax.numpy as jnp
from jax import lax

D = 4096
K = 128
ROWS_ALL = 262144


def draw_data(key, part):
    key = jax.random.fold_in(key, 7)
    key_base = jax.random.fold_in(key, 1)
    key_rows = jax.random.fold_in(key, 2)
    key_cols = jax.random.fold_in(key, 3)
    base = jax.random.normal(key_base, (ROWS_ALL, D), jnp.float32)
    row_scale = jnp.exp(jax.random.uniform(key_rows, (ROWS_ALL, 1), jnp.float32, 0.0, 2.3025851))
    col_scale = jnp.exp(jax.random.uniform(key_cols, (1, D), jnp.float32, 0.0, 1.0986123))
    return (base * row_scale * col_scale).astype(jnp.bfloat16)


def bell_draw(key, shape, scale, most, dtype=jnp.bfloat16):
    entries = jax.random.normal(key, shape, jnp.float32) * scale
    return jnp.minimum(jnp.maximum(entries, -most), most).astype(dtype)


def setup_inputs(seed: int = 0) -> dict:
    keys = jax.random.split(jax.random.key(seed), 3)
    data = draw_data(jax.random.fold_in(keys[2], 71), 0)
    sketch = bell_draw(keys[1], (D, K), D ** -0.5, 0.09375)
    return {"data": data, "sketch": sketch}


def orthonormal(block):
    gram = lax.dot_general(block.astype(jnp.float32), block.astype(jnp.float32), (((0,), (0,)), ((), ())), precision=lax.Precision.HIGHEST, preferred_element_type=jnp.float32)
    lower = jnp.linalg.cholesky(gram)
    return lax.linalg.triangular_solve(lower, block, left_side=False, lower=True, transpose_a=True)

def reference(data, sketch):
    first = jnp.dot(data.astype(jnp.float32), sketch.astype(jnp.float32), preferred_element_type=jnp.float32)
    range_first = orthonormal(first)
    first_basis = jnp.sqrt(jnp.float32(ROWS_ALL)) * range_first
    range_low = range_first.astype(jnp.bfloat16)
    back = lax.dot_general(range_low.astype(jnp.float32), data.astype(jnp.float32), (((0,), (0,)), ((), ())), preferred_element_type=jnp.float32)
    back_low = (back / jnp.sqrt(jnp.float32(ROWS_ALL))).astype(jnp.bfloat16)
    second = lax.dot_general(data.astype(jnp.float32), back_low.astype(jnp.float32), (((1,), (1,)), ((), ())), preferred_element_type=jnp.float32)
    range_second = orthonormal(second)
    basis = jnp.sqrt(jnp.float32(ROWS_ALL)) * range_second
    second_low = range_second.astype(jnp.bfloat16)
    terms = lax.dot_general(second_low.astype(jnp.float32), data.astype(jnp.float32), (((0,), (0,)), ((), ())), preferred_element_type=jnp.float32)
    projected = jnp.sqrt(jnp.float32(D) / jnp.float32(ROWS_ALL)) * terms
    return (first_basis, basis, projected)
```

```python
import jax
import jax.numpy as jnp
from jax import lax
from jax.sharding import Mesh, PartitionSpec as P

D = 4096
K = 128
Z, X, C, Y = 8, 4, 2, 4
AXES = ("z", "x", "core", "y")
PLANE = X * Y
WIDE = D // C // PLANE
THIN = K // C // PLANE


def device_number(z, x, core, y):
    return ((z * X + x) * C + core) * Y + y


def exchange(value, partner):
    pairs = []
    for z in range(Z):
        for x in range(X):
            for core in range(C):
                for y in range(Y):
                    pairs.append((device_number(z, x, core, y), device_number(*partner(z, x, core, y))))
    return lax.ppermute(value, AXES, pairs)


def other_core(value):
    return exchange(value, lambda z, x, core, y: (z, x, 1 - core, y))


def sum_everywhere(value):
    core = lax.axis_index("core")
    give = lax.dynamic_index_in_dim(value, 1 - core, keepdims=False)
    keep = lax.dynamic_index_in_dim(value, core, keepdims=False)
    half = keep + other_core(give)
    part = lax.all_to_all(half, ("x", "y"), split_axis=0, concat_axis=0, tiled=True)
    part = jnp.sum(part, axis=0)
    for mask in (1, 3, 7):
        part = part + exchange(part, lambda z, x, core, y: (z ^ mask, x, core, y))
    half = lax.all_to_all(
        jnp.broadcast_to(part, (PLANE,) + part.shape), ("x", "y"), split_axis=0, concat_axis=0, tiled=True
    )
    other = other_core(half)
    return jnp.where(core == 0, jnp.stack([half, other]), jnp.stack([other, half]))


def exact_dot(left, right, dims):
    return lax.dot_general(
        left, right, (dims, ((), ())), precision=lax.Precision.HIGHEST, preferred_element_type=jnp.float32
    )


def products(data, block):
    gram = exact_dot(block, block, ((0,), (0,)))
    high = block.astype(jnp.bfloat16)
    low = (block - high.astype(jnp.float32)).astype(jnp.bfloat16)
    both = lax.dot_general(
        jnp.concatenate([high, low], axis=1), data, (((0,), (0,)), ((), ())), preferred_element_type=jnp.float32
    )
    terms = both[:K] + both[K:]
    terms = terms.reshape(K, C, PLANE, WIDE).transpose(1, 2, 0, 3)
    gram = gram.reshape(C, PLANE, THIN, K)
    total = sum_everywhere(jnp.concatenate([terms, gram], axis=2))
    terms = total[:, :, :K].transpose(2, 0, 1, 3).reshape(K, D)
    gram = total[:, :, K:].reshape(K, K)
    lower = jnp.linalg.cholesky(gram)
    inverse = lax.linalg.triangular_solve(lower, jnp.eye(K, dtype=jnp.float32), left_side=True, lower=True)
    return terms, inverse


def on_device(data, sketch):
    row_count = data.shape[0] * Z * X * C * Y
    root_rows = jnp.sqrt(jnp.float32(row_count))
    first = jnp.dot(data, sketch, preferred_element_type=jnp.float32)
    terms, inverse = products(data, first)
    first_basis = exact_dot(first, root_rows * inverse, ((1,), (1,)))
    back_low = (exact_dot(inverse, terms, ((1,), (0,))) / root_rows).astype(jnp.bfloat16)
    second = lax.dot_general(data, back_low, (((1,), (1,)), ((), ())), preferred_element_type=jnp.float32)
    terms, inverse = products(data, second)
    basis = exact_dot(second, root_rows * inverse, ((1,), (1,)))
    scale = jnp.sqrt(jnp.float32(D) / jnp.float32(row_count))
    projected = exact_dot(scale * inverse, terms, ((1,), (0,)))
    return (first_basis, basis, projected)


def solution(mesh):
    split = Mesh(mesh.devices.reshape(Z, X, C, Y), AXES)
    return jax.shard_map(
        on_device,
        mesh=split,
        in_specs=(P(AXES, None), P()),
        out_specs=(P(AXES, None), P(AXES, None), P()),
        check_vma=False,
    )
```

```python
import functools

import jax
import jax.numpy as jnp
from jax import lax
from jax.experimental import pallas as pl
from jax.experimental.pallas import tpu as pltpu
from jax.sharding import Mesh, PartitionSpec as P

D = 4096
K = 128
Z, X, C, Y = 8, 4, 2, 4
AXES = ("z", "x", "core", "y")
PLANE = X * Y
HALF = D // C
WIDE = HALF // PLANE
THIN = K // PLANE
ROWS = K + THIN
ROOT_ROWS = 512.0
BLOCK = 256
STEPS = 4
VMEM = 48 * 2**20


def device_number(z, x, core, y):
    return ((z * X + x) * C + core) * Y + y


def exchange(value, partner):
    pairs = []
    for z in range(Z):
        for x in range(X):
            for core in range(C):
                for y in range(Y):
                    pairs.append((device_number(z, x, core, y), device_number(*partner(z, x, core, y))))
    return lax.ppermute(value, AXES, pairs)


def other_core(value):
    return exchange(value, lambda z, x, core, y: (z, x, 1 - core, y))


def sum_everywhere(give, keep):
    half = keep + other_core(give)
    part = lax.all_to_all(half, ("x", "y"), split_axis=0, concat_axis=0, tiled=True)
    part = jnp.sum(part, axis=0)
    for mask in (1, 3, 7):
        part = part + exchange(part, lambda z, x, core, y: (z ^ mask, x, core, y))
    half = lax.all_to_all(
        jnp.broadcast_to(part, (PLANE,) + part.shape), ("x", "y"), split_axis=0, concat_axis=0, tiled=True
    )
    return half, other_core(half)


def exact_dot(left, right, dims):
    return lax.dot_general(
        left, right, (dims, ((), ())), precision=lax.Precision.HIGHEST, preferred_element_type=jnp.float32
    )


def quick_dot(left, right, dims=((1,), (0,))):
    return lax.dot_general(left, right, (dims, ((), ())), preferred_element_type=jnp.float32)


def two_terms(value):
    high = value.astype(jnp.bfloat16)
    return high, (value - high.astype(jnp.float32)).astype(jnp.bfloat16)


def inverse_factor(gram):
    row = lax.broadcasted_iota(jnp.int32, (K, K), 0)
    column = lax.broadcasted_iota(jnp.int32, (K, K), 1)
    diagonal = jnp.where(row == column, gram, 0.0)
    across = lax.rsqrt(jnp.sum(diagonal, axis=0, keepdims=True))
    down = lax.rsqrt(jnp.sum(diagonal, axis=1, keepdims=True))
    scaled = gram * across * down
    groups = [scaled[8 * g : 8 * g + 8] for g in range(K // 8)]
    lane = lax.broadcasted_iota(jnp.int32, (8, K), 1)
    sub = lax.broadcasted_iota(jnp.int32, (8, K), 0)

    def spread(value, k):
        return jnp.broadcast_to(value[:, k : k + 1], (8, K))

    for k in range(0, K, 4):
        g0, off = k // 8, k % 8
        mine = groups[g0]
        raw = [jnp.broadcast_to(mine[off + t : off + t + 1], (8, K)) for t in range(4)]
        s = {(i, j): spread(raw[i], k + j) for i in range(4) for j in range(i + 1)}
        inside = (lane >= k) & (lane < k + 4)
        e = [jnp.where(inside, jnp.where(lane == k + t, 1.0, 0.0), raw[t]) for t in range(4)]
        a, b, c = s[0, 0], s[1, 0], s[1, 1]
        turn = 1.0 / (a * c - b * b)
        ca, cb, cc = a * turn, b * turn, c * turn
        u0 = cc * e[0] - cb * e[1]
        u1 = ca * e[1] - cb * e[0]
        v20 = cc * s[2, 0] - cb * s[2, 1]
        v21 = ca * s[2, 1] - cb * s[2, 0]
        v30 = cc * s[3, 0] - cb * s[3, 1]
        v31 = ca * s[3, 1] - cb * s[3, 0]
        p = s[2, 2] - s[2, 0] * v20 - s[2, 1] * v21
        q = s[3, 2] - s[3, 0] * v20 - s[3, 1] * v21
        r = s[3, 3] - s[3, 0] * v30 - s[3, 1] * v31
        e2 = e[2] - s[2, 0] * u0 - s[2, 1] * u1
        e3 = e[3] - s[3, 0] * u0 - s[3, 1] * u1
        turn = 1.0 / (p * r - q * q)
        u2 = (r * turn) * e2 - (q * turn) * e3
        u3 = (p * turn) * e3 - (q * turn) * e2
        u0 = u0 - v20 * u2 - v30 * u3
        u1 = u1 - v21 * u2 - v31 * u3
        upper, lower = b / a, q / p
        done = [
            e[0] * lax.rsqrt(a),
            (e[1] - upper * e[0]) * lax.rsqrt(c - upper * b),
            e2 * lax.rsqrt(p),
            (e3 - lower * e2) * lax.rsqrt(r - lower * q),
        ]
        for g in range(g0 + (off == 4), K // 8):
            value = groups[g]
            change = spread(value, k) * u0 + spread(value, k + 1) * u1
            change = change + spread(value, k + 2) * u2 + spread(value, k + 3) * u3
            groups[g] = jnp.where(inside, 0.0, value) - change
        value = groups[g0]
        for t in range(4):
            value = jnp.where(sub == off + t, done[t], value)
        groups[g0] = value
    full = jnp.concatenate(groups, axis=0)
    return jnp.where(row >= column, full, 0.0) * across


def add_rows(block, part, gram, total):
    gram[...] += exact_dot(part, part, ((0,), (0,)))
    high, low = two_terms(part)
    both = jnp.concatenate([high, low], axis=1).T
    total[...] += quick_dot(both, block)


def clear(gram, total):
    gram[...] = jnp.zeros_like(gram)
    total[...] = jnp.zeros_like(total)


def hand_over(core, gram, total, give, keep):
    for ref, start in ((give, (1 - core) * HALF), (keep, core * HALF)):
        for j in range(PLANE):
            columns = pl.ds(pl.multiple_of(start + WIDE * j, WIDE), WIDE)
            ref[j, :K, :] = total[:K, columns] + total[K:, columns]
            ref[j, K:, :] = gram[THIN * j : THIN * (j + 1), :]


def start_kernel(core, data, sketch, first, give, keep, gram, total):
    step = pl.program_id(0)

    @pl.when(step == 0)
    def _():
        clear(gram, total)

    part = quick_dot(data[...], sketch[...])
    first[...] = part
    add_rows(data[...], part, gram, total)

    @pl.when(step == STEPS - 1)
    def _():
        hand_over(core[0], gram, total, give, keep)


def all_terms(core, own, other):
    for ref, start in ((own, core * HALF), (other, (1 - core) * HALF)):
        for j in range(0, PLANE, 2):
            yield pl.multiple_of(start + WIDE * j, 2 * WIDE), jnp.concatenate([ref[j, :K, :], ref[j + 1, :K, :]], axis=1)


def apply_factor(inverse, terms):
    high, low = two_terms(inverse)
    left = jnp.concatenate(
        [jnp.concatenate([high, high], axis=1), jnp.concatenate([low, jnp.zeros_like(low)], axis=1)], axis=0
    )
    both = quick_dot(left, jnp.concatenate(two_terms(terms), axis=0))
    return both[:K] + both[K:]


def summed_gram(own):
    return jnp.concatenate([own[j, K:, :] for j in range(PLANE)], axis=0)


def middle_kernel(core, own, other, data, inverse, second, give, keep, held, back, gram, total, arrived):
    copies = [
        pltpu.make_async_copy(data.at[pl.ds(b * BLOCK, BLOCK)], held.at[pl.ds(b * BLOCK, BLOCK)], arrived.at[b])
        for b in range(STEPS)
    ]
    for copy in copies:
        copy.start()
    clear(gram, total)
    inverse[...] = inverse_factor(summed_gram(own))
    scaled = inverse[...] * (1.0 / ROOT_ROWS)
    for start, terms in all_terms(core[0], own, other):
        back[:, pl.ds(start, 2 * WIDE)] = apply_factor(scaled, terms).astype(jnp.bfloat16)
    for b in range(STEPS):
        copies[b].wait()
        rows = pl.ds(b * BLOCK, BLOCK)
        part = quick_dot(held[rows, :], back[...], ((1,), (1,)))
        second[rows, :] = part
        add_rows(held[rows, :], part, gram, total)
    hand_over(core[0], gram, total, give, keep)


def final_kernel(core, own, other, inverse, projected):
    inverse[...] = inverse_factor(summed_gram(own))
    scaled = inverse[...] * (D**0.5 / ROOT_ROWS)
    for start, terms in all_terms(core[0], own, other):
        projected[:, pl.ds(start, 2 * WIDE)] = apply_factor(scaled, terms)


def params():
    return pltpu.CompilerParams(vmem_limit_bytes=VMEM)


VM = pl.BlockSpec(memory_space=pltpu.VMEM)
SM = pl.BlockSpec(memory_space=pltpu.SMEM)
MESSAGE = jax.ShapeDtypeStruct((PLANE, ROWS, K), jnp.float32)
SQUARE = jax.ShapeDtypeStruct((K, K), jnp.float32)
SUMS = [pltpu.VMEM((K, K), jnp.float32), pltpu.VMEM((2 * K, D), jnp.float32)]


def start_call(core, data, sketch):
    tall = jax.ShapeDtypeStruct((data.shape[0], K), jnp.float32)
    whole = pl.BlockSpec((PLANE, ROWS, K), lambda i: (0, 0, 0))
    return pl.pallas_call(
        start_kernel,
        grid=(STEPS,),
        out_shape=(tall, MESSAGE, MESSAGE),
        in_specs=[SM, pl.BlockSpec((BLOCK, D), lambda i: (i, 0)), pl.BlockSpec((D, K), lambda i: (0, 0))],
        out_specs=(pl.BlockSpec((BLOCK, K), lambda i: (i, 0)), whole, whole),
        scratch_shapes=SUMS,
        compiler_params=params(),
        name="start",
    )(core, data, sketch)


def middle_call(core, own, other, data):
    tall = jax.ShapeDtypeStruct((data.shape[0], K), jnp.float32)
    return pl.pallas_call(
        middle_kernel,
        out_shape=(SQUARE, tall, MESSAGE, MESSAGE),
        in_specs=[SM, VM, VM, pl.BlockSpec(memory_space=pl.ANY)],
        out_specs=(VM, VM, VM, VM),
        scratch_shapes=[pltpu.VMEM(data.shape, jnp.bfloat16), pltpu.VMEM((K, D), jnp.bfloat16)]
        + SUMS
        + [pltpu.SemaphoreType.DMA((STEPS,))],
        compiler_params=params(),
        name="middle",
    )(core, own, other, data)


def final_call(core, own, other):
    return pl.pallas_call(
        final_kernel,
        out_shape=(SQUARE, jax.ShapeDtypeStruct((K, D), jnp.float32)),
        in_specs=[SM, VM, VM],
        out_specs=(VM, VM),
        compiler_params=params(),
        name="final",
    )(core, own, other)


def on_device(data, sketch):
    core = lax.axis_index("core").astype(jnp.int32).reshape(1)
    first, give, keep = start_call(core, data, sketch)
    own, other = sum_everywhere(give, keep)
    inverse, second, give, keep = middle_call(core, own, other, data)
    first_basis = exact_dot(first, ROOT_ROWS * inverse, ((1,), (1,)))
    own, other = sum_everywhere(give, keep)
    inverse, projected = final_call(core, own, other)
    basis = exact_dot(second, ROOT_ROWS * inverse, ((1,), (1,)))
    return (first_basis, basis, projected)


def solution(mesh):
    split = Mesh(mesh.devices.reshape(Z, X, C, Y), AXES)
    return jax.shard_map(
        on_device,
        mesh=split,
        in_specs=(P(AXES, None), P()),
        out_specs=(P(AXES, None), P(AXES, None), P()),
        check_vma=False,
    )
```

```python
import jax
import jax.numpy as jnp
from jax import lax
from jax.experimental import pallas as pl
from jax.experimental.pallas import tpu as pltpu
from jax.sharding import Mesh, PartitionSpec as P

D = 4096
K = 128
Z, X, C, Y = 8, 4, 2, 4
AXES = ("z", "x", "core", "y")
PLANE = X * Y
HALF = D // C
WIDE = HALF // PLANE
THIN = K // PLANE
ROWS = K + THIN
ROOT_ROWS = 512.0
BLOCK = 256
COLUMNS = 512
STEPS = 4
VMEM = 48 * 2**20


def device_number(z, x, core, y):
    return ((z * X + x) * C + core) * Y + y


def exchange(value, partner):
    pairs = []
    for z in range(Z):
        for x in range(X):
            for core in range(C):
                for y in range(Y):
                    pairs.append((device_number(z, x, core, y), device_number(*partner(z, x, core, y))))
    return lax.ppermute(value, AXES, pairs)


def other_core(value):
    return exchange(value, lambda z, x, core, y: (z, x, 1 - core, y))


def sum_everywhere(give, keep):
    half = keep + other_core(give)
    part = lax.all_to_all(half, ("x", "y"), split_axis=0, concat_axis=0, tiled=True)
    part = jnp.sum(part, axis=0)
    for mask in (1, 2, 6):
        part = part + exchange(part, lambda z, x, core, y: (z ^ mask, x, core, y))
    half = lax.all_to_all(
        jnp.broadcast_to(part, (PLANE,) + part.shape), ("x", "y"), split_axis=0, concat_axis=0, tiled=True
    )
    return half, other_core(half)


def exact_dot(left, right, dims):
    return lax.dot_general(
        left, right, (dims, ((), ())), precision=lax.Precision.HIGHEST, preferred_element_type=jnp.float32
    )


def quick_dot(left, right, dims=((1,), (0,))):
    return lax.dot_general(left, right, (dims, ((), ())), preferred_element_type=jnp.float32)


def two_terms(value):
    high = value.astype(jnp.bfloat16)
    return high, (value - high.astype(jnp.float32)).astype(jnp.bfloat16)


def reciprocal(value):
    rough = pl.reciprocal(value, approx=True)
    return rough * (2.0 - value * rough)


def inverse_factor(gram):
    row = lax.broadcasted_iota(jnp.int32, (K, K), 0)
    column = lax.broadcasted_iota(jnp.int32, (K, K), 1)
    diagonal = jnp.where(row == column, gram, 0.0)
    across = lax.rsqrt(jnp.sum(diagonal, axis=0, keepdims=True))
    down = lax.rsqrt(jnp.sum(diagonal, axis=1, keepdims=True))
    scaled = gram * across * down
    groups = [scaled[8 * g : 8 * g + 8] for g in range(K // 8)]
    lane = lax.broadcasted_iota(jnp.int32, (8, K), 1)
    sub = lax.broadcasted_iota(jnp.int32, (8, K), 0)

    def spread(value, k):
        return jnp.broadcast_to(value[:, k : k + 1], (8, K))

    for g0 in range(K // 8):
        k = 8 * g0
        mine = groups[g0]
        columns = [spread(mine, k + t) for t in range(8)]
        s = {(i, j): jnp.broadcast_to(columns[j][i : i + 1], (8, K)) for i in range(8) for j in range(i + 1)}
        inside = (lane >= k) & (lane < k + 8)
        e = [
            jnp.where(inside, jnp.where(lane == k + t, 1.0, 0.0), jnp.broadcast_to(mine[t : t + 1], (8, K)))
            for t in range(8)
        ]
        u, v, done = [None] * 8, {}, [None] * 8
        for h in (0, 2, 4, 6):
            a, b, c = s[h, h], s[h + 1, h], s[h + 1, h + 1]
            turn = reciprocal(a * c - b * b)
            n0, n1 = c * e[h] - b * e[h + 1], a * e[h + 1] - b * e[h]
            root = lax.rsqrt(a)
            ratio = b * (root * root)
            done[h] = e[h] * root
            done[h + 1] = (e[h + 1] - ratio * e[h]) * lax.rsqrt(c - ratio * b)
            u[h], u[h + 1] = n0 * turn, n1 * turn
            m = {}
            for i in range(h + 2, 8):
                m[i] = (c * s[i, h] - b * s[i, h + 1], a * s[i, h + 1] - b * s[i, h])
                v[i, h] = (m[i][0] * turn, m[i][1] * turn)
                e[i] = e[i] - (s[i, h] * n0 + s[i, h + 1] * n1) * turn
                for j in range(h + 2, i + 1):
                    s[i, j] = s[i, j] - (s[i, h] * m[j][0] + s[i, h + 1] * m[j][1]) * turn
        for h in (4, 2, 0):
            for i in range(h + 2, 8):
                u[h] = u[h] - v[i, h][0] * u[i]
                u[h + 1] = u[h + 1] - v[i, h][1] * u[i]
        for g in range(g0 + 1, K // 8):
            value = jnp.where(inside, 0.0, groups[g])
            for t in (6, 4, 2, 0):
                value = value - (spread(groups[g], k + t) * u[t] + spread(groups[g], k + t + 1) * u[t + 1])
            groups[g] = value
        value = done[0]
        for t in range(1, 8):
            value = jnp.where(sub == t, done[t], value)
        groups[g0] = value
    full = jnp.concatenate(groups, axis=0)
    return jnp.where(row >= column, full, 0.0) * across


def three_term_gram(block):
    high, low = two_terms(block)
    rest = (block - high.astype(jnp.float32) - low.astype(jnp.float32)).astype(jnp.bfloat16)
    both = jnp.concatenate([high, low], axis=1)
    main = quick_dot(both, both, ((0,), (0,)))
    side = quick_dot(high, rest, ((0,), (0,)))
    return main[:K, :K] + (main[:K, K:] + main[K:, :K]) + (main[K:, K:] + side + side.T)


def apply_factor(inverse, terms):
    high, low = two_terms(inverse)
    left = jnp.concatenate(
        [jnp.concatenate([high, high], axis=1), jnp.concatenate([low, jnp.zeros_like(low)], axis=1)], axis=0
    )
    both = quick_dot(left, jnp.concatenate(two_terms(terms), axis=0))
    return both[:K] + both[K:]


def apply_everywhere(core, own, other, inverse, store):
    def step(n, _):
        for ref, start in ((own, core * HALF), (other, (1 - core) * HALF)):
            terms = jnp.concatenate([ref[2 * n, :K, :], ref[2 * n + 1, :K, :]], axis=1)
            store(pl.multiple_of(start + 2 * WIDE * n, 2 * WIDE), apply_factor(inverse, terms))
        return 0

    lax.fori_loop(0, PLANE // 2, step, 0)


def fetch(data, held, arrived):
    copies = [
        pltpu.make_async_copy(data.at[pl.ds(b * BLOCK, BLOCK)], held.at[pl.ds(b * BLOCK, BLOCK)], arrived.at[b])
        for b in range(STEPS)
    ]
    for copy in copies:
        copy.start()
    return copies


def make_message(core, held, tall, give, keep, turned):
    gram = three_term_gram(tall[...])
    for j in range(PLANE):
        rows = gram[THIN * j : THIN * (j + 1), :]
        give[j, K:, :] = rows
        keep[j, K:, :] = rows
    turned[...] = jnp.concatenate(two_terms(tall[...]), axis=1).T

    def step(n, _):
        for ref, start in ((give, (1 - core) * HALF), (keep, core * HALF)):
            columns = pl.ds(pl.multiple_of(start + COLUMNS * n, COLUMNS), COLUMNS)
            both = quick_dot(turned[...], held[:, columns])
            terms = both[:K] + both[K:]
            for i in range(COLUMNS // WIDE):
                ref[COLUMNS // WIDE * n + i, :K, :] = terms[:, WIDE * i : WIDE * (i + 1)]
        return 0

    lax.fori_loop(0, HALF // COLUMNS, step, 0)


def start_kernel(core, data, sketch, first, give, keep, held, weights, turned, arrived, ready):
    copies = fetch(data, held, arrived)
    get = pltpu.make_async_copy(sketch, weights, ready)
    get.start()
    get.wait()
    for b in range(STEPS):
        copies[b].wait()
        rows = pl.ds(b * BLOCK, BLOCK)
        first[rows, :] = quick_dot(held[rows, :], weights[...])
    make_message(core[0], held, first, give, keep, turned)


def factor_kernel(own, inverse):
    inverse[...] = inverse_factor(jnp.concatenate([own[j, K:, :] for j in range(PLANE)], axis=0))


def middle_kernel(core, own, other, inverse, data, second, give, keep, held, back, turned, arrived):
    copies = fetch(data, held, arrived)
    scaled = inverse[...] * (1.0 / ROOT_ROWS)

    def store(start, terms):
        back[:, pl.ds(start, 2 * WIDE)] = terms.astype(jnp.bfloat16)

    apply_everywhere(core[0], own, other, scaled, store)
    for b in range(STEPS):
        copies[b].wait()
        rows = pl.ds(b * BLOCK, BLOCK)
        second[rows, :] = quick_dot(held[rows, :], back[...], ((1,), (1,)))
    make_message(core[0], held, second, give, keep, turned)


def final_kernel(core, own, other, inverse, tall, projected, basis):
    scaled = inverse[...] * (D**0.5 / ROOT_ROWS)

    def store(start, terms):
        projected[:, pl.ds(start, 2 * WIDE)] = terms

    apply_everywhere(core[0], own, other, scaled, store)
    basis[...] = exact_dot(tall[...], inverse[...] * ROOT_ROWS, ((1,), (1,)))


def params():
    return pltpu.CompilerParams(vmem_limit_bytes=VMEM)


VM = pl.BlockSpec(memory_space=pltpu.VMEM)
SM = pl.BlockSpec(memory_space=pltpu.SMEM)
ANY = pl.BlockSpec(memory_space=pl.ANY)
MESSAGE = jax.ShapeDtypeStruct((PLANE, ROWS, K), jnp.float32)
SQUARE = jax.ShapeDtypeStruct((K, K), jnp.float32)


def start_call(core, data, sketch):
    rows = data.shape[0]
    return pl.pallas_call(
        start_kernel,
        out_shape=(jax.ShapeDtypeStruct((rows, K), jnp.float32), MESSAGE, MESSAGE),
        in_specs=[SM, ANY, ANY],
        out_specs=(VM, VM, VM),
        scratch_shapes=[
            pltpu.VMEM(data.shape, jnp.bfloat16),
            pltpu.VMEM(sketch.shape, jnp.bfloat16),
            pltpu.VMEM((2 * K, rows), jnp.bfloat16),
            pltpu.SemaphoreType.DMA((STEPS,)),
            pltpu.SemaphoreType.DMA,
        ],
        compiler_params=params(),
        name="start",
    )(core, data, sketch)


def factor_call(own):
    return pl.pallas_call(
        factor_kernel,
        out_shape=SQUARE,
        in_specs=[VM],
        out_specs=VM,
        compiler_params=params(),
        cost_estimate=pl.CostEstimate(flops=K**3, bytes_accessed=10**6, transcendentals=0),
        name="factor",
    )(own)


def middle_call(core, own, other, inverse, data):
    rows = data.shape[0]
    return pl.pallas_call(
        middle_kernel,
        out_shape=(jax.ShapeDtypeStruct((rows, K), jnp.float32), MESSAGE, MESSAGE),
        in_specs=[SM, VM, VM, VM, ANY],
        out_specs=(VM, VM, VM),
        scratch_shapes=[
            pltpu.VMEM(data.shape, jnp.bfloat16),
            pltpu.VMEM((K, D), jnp.bfloat16),
            pltpu.VMEM((2 * K, rows), jnp.bfloat16),
            pltpu.SemaphoreType.DMA((STEPS,)),
        ],
        compiler_params=params(),
        name="middle",
    )(core, own, other, inverse, data)


def final_call(core, own, other, inverse, tall):
    return pl.pallas_call(
        final_kernel,
        out_shape=(jax.ShapeDtypeStruct((K, D), jnp.float32), jax.ShapeDtypeStruct(tall.shape, jnp.float32)),
        in_specs=[SM, VM, VM, VM, VM],
        out_specs=(VM, VM),
        compiler_params=params(),
        name="final",
    )(core, own, other, inverse, tall)


def on_device(data, sketch):
    core = lax.axis_index("core").astype(jnp.int32).reshape(1)
    first, give, keep = start_call(core, data, sketch)
    own, other = sum_everywhere(give, keep)
    inverse = factor_call(own)
    second, give, keep = middle_call(core, own, other, inverse, data)
    first_basis = exact_dot(first, ROOT_ROWS * inverse, ((1,), (1,)))
    own, other = sum_everywhere(give, keep)
    inverse = factor_call(own)
    projected, basis = final_call(core, own, other, inverse, second)
    return (first_basis, basis, projected)


def solution(mesh):
    split = Mesh(mesh.devices.reshape(Z, X, C, Y), AXES)
    return jax.shard_map(
        on_device,
        mesh=split,
        in_specs=(P(AXES, None), P()),
        out_specs=(P(AXES, None), P(AXES, None), P()),
        check_vma=False,
    )
```

```python
import jax
import jax.numpy as jnp
from jax import lax
from jax.experimental import pallas as pl
from jax.experimental.pallas import tpu as pltpu
from jax.sharding import Mesh, PartitionSpec as P

D = 4096
K = 128
Z, X, C, Y = 8, 4, 2, 4
AXES = ("z", "x", "core", "y")
PLANE = X * Y
HALF = D // C
WIDE = HALF // PLANE
THIN = K // PLANE
ROWS = K + THIN
ROOT_ROWS = 512.0
BLOCK = 256
STEPS = 4


def device_number(z, x, core, y):
    return ((z * X + x) * C + core) * Y + y


def exchange(value, partner):
    pairs = []
    for z in range(Z):
        for x in range(X):
            for core in range(C):
                for y in range(Y):
                    pairs.append((device_number(z, x, core, y), device_number(*partner(z, x, core, y))))
    return lax.ppermute(value, AXES, pairs)


def other_core(value):
    return exchange(value, lambda z, x, core, y: (z, x, 1 - core, y))


def plane_partner(mask, first):
    def partner(z, x, core, y):
        return (z, x, core, y ^ mask) if (core == 0) == first else (z, x ^ mask, core, y)

    return partner


def sum_everywhere(give, keep, beside=()):
    half = keep + other_core(give)
    for first in (True, False):
        half = half.reshape((4, -1) + half.shape[1:])
        arrived = [exchange(half[mask], plane_partner(mask, first)) for mask in (2, 1, 3)]
        half = half[0] + arrived[0] + arrived[1] + arrived[2]
    part = half[0]
    arrived = [exchange(part, lambda z, x, core, y: (z ^ mask, x, core, y)) for mask in (3, 2, 1)]
    arrived, beside = lax.optimization_barrier((arrived, beside))
    part = part + arrived[0] + arrived[1] + arrived[2]
    part = part + exchange(part, lambda z, x, core, y: (z ^ 6, x, core, y))
    own = lax.all_to_all(
        jnp.broadcast_to(part, (PLANE,) + part.shape), ("x", "y"), split_axis=0, concat_axis=0, tiled=True
    )
    return own, other_core(own), beside


def exact_dot(left, right, dims):
    return lax.dot_general(
        left, right, (dims, ((), ())), precision=lax.Precision.HIGHEST, preferred_element_type=jnp.float32
    )


def quick_dot(left, right, dims=((1,), (0,))):
    return lax.dot_general(left, right, (dims, ((), ())), preferred_element_type=jnp.float32)


def two_terms(value):
    high = value.astype(jnp.bfloat16)
    return high, (value - high.astype(jnp.float32)).astype(jnp.bfloat16)


def reciprocal(value):
    rough = pl.reciprocal(value, approx=True)
    return rough * (2.0 - value * rough)


def inverse_factor(gram):
    row = lax.broadcasted_iota(jnp.int32, (K, K), 0)
    column = lax.broadcasted_iota(jnp.int32, (K, K), 1)
    diagonal = jnp.where(row == column, gram, 0.0)
    across = lax.rsqrt(jnp.sum(diagonal, axis=0, keepdims=True))
    down = lax.rsqrt(jnp.sum(diagonal, axis=1, keepdims=True))
    scaled = gram * across * down
    groups = [scaled[8 * g : 8 * g + 8] for g in range(K // 8)]
    lane = lax.broadcasted_iota(jnp.int32, (8, K), 1)
    sub = lax.broadcasted_iota(jnp.int32, (8, K), 0)

    def spread(value, k):
        return jnp.broadcast_to(value[:, k : k + 1], (8, K))

    for g0 in range(K // 8):
        k = 8 * g0
        mine = groups[g0]
        columns = [spread(mine, k + t) for t in range(8)]
        s = {(i, j): jnp.broadcast_to(columns[j][i : i + 1], (8, K)) for i in range(8) for j in range(i + 1)}
        inside = (lane >= k) & (lane < k + 8)
        e = [
            jnp.where(inside, jnp.where(lane == k + t, 1.0, 0.0), jnp.broadcast_to(mine[t : t + 1], (8, K)))
            for t in range(8)
        ]
        u, v, done = [None] * 8, {}, [None] * 8
        for h in (0, 2, 4, 6):
            a, b, c = s[h, h], s[h + 1, h], s[h + 1, h + 1]
            turn = reciprocal(a * c - b * b)
            n0, n1 = c * e[h] - b * e[h + 1], a * e[h + 1] - b * e[h]
            root = lax.rsqrt(a)
            ratio = b * (root * root)
            done[h] = e[h] * root
            done[h + 1] = (e[h + 1] - ratio * e[h]) * lax.rsqrt(c - ratio * b)
            u[h], u[h + 1] = n0 * turn, n1 * turn
            m = {}
            for i in range(h + 2, 8):
                m[i] = (c * s[i, h] - b * s[i, h + 1], a * s[i, h + 1] - b * s[i, h])
                v[i, h] = (m[i][0] * turn, m[i][1] * turn)
                e[i] = e[i] - (s[i, h] * n0 + s[i, h + 1] * n1) * turn
                for j in range(h + 2, i + 1):
                    s[i, j] = s[i, j] - (s[i, h] * m[j][0] + s[i, h + 1] * m[j][1]) * turn
        for h in (4, 2, 0):
            for i in range(h + 2, 8):
                u[h] = u[h] - v[i, h][0] * u[i]
                u[h + 1] = u[h + 1] - v[i, h][1] * u[i]
        for g in range(g0 + 1, K // 8):
            value = jnp.where(inside, 0.0, groups[g])
            for t in (6, 4, 2, 0):
                value = value - (spread(groups[g], k + t) * u[t] + spread(groups[g], k + t + 1) * u[t + 1])
            groups[g] = value
        value = done[0]
        for t in range(1, 8):
            value = jnp.where(sub == t, done[t], value)
        groups[g0] = value
    full = jnp.concatenate(groups, axis=0)
    return jnp.where(row >= column, full, 0.0) * across


def three_term_gram(block):
    high, low = two_terms(block)
    rest = (block - high.astype(jnp.float32) - low.astype(jnp.float32)).astype(jnp.bfloat16)
    both = jnp.concatenate([high, low], axis=1)
    main = quick_dot(both, both, ((0,), (0,)))
    side = quick_dot(high, rest, ((0,), (0,)))
    return main[:K, :K] + (main[:K, K:] + main[K:, :K]) + (main[K:, K:] + side + side.T)


def apply_factor(inverse, terms):
    high, low = two_terms(inverse)
    left = jnp.concatenate(
        [jnp.concatenate([high, high], axis=1), jnp.concatenate([low, jnp.zeros_like(low)], axis=1)], axis=0
    )
    both = quick_dot(left, jnp.concatenate(two_terms(terms), axis=0))
    return both[:K] + both[K:]


def apply_everywhere(core, own, other, inverse, store):
    for n in range(PLANE // 2):
        for ref, start in ((own, core * HALF), (other, (1 - core) * HALF)):
            terms = jnp.concatenate([ref[2 * n, :K, :], ref[2 * n + 1, :K, :]], axis=1)
            store(pl.multiple_of(start + 2 * WIDE * n, 2 * WIDE), apply_factor(inverse, terms))


def fetch(data, held, arrived):
    copies = [
        pltpu.make_async_copy(data.at[pl.ds(b * BLOCK, BLOCK)], held.at[pl.ds(b * BLOCK, BLOCK)], arrived.at[b])
        for b in range(STEPS)
    ]
    for copy in copies:
        copy.start()
    return copies


def make_message(place, held, tall, give, keep, turned):
    core, x, y = place
    sides = ((give, 1 - core), (keep, core))

    def slot(side, at_x, at_y):
        over_x, over_y = at_x ^ x, at_y ^ y
        return jnp.where(side == 0, 4 * over_y + over_x, 4 * over_x + over_y)

    gram = three_term_gram(tall[...])
    for j in range(PLANE):
        for ref, side in sides:
            ref[slot(side, j // Y, j % Y), K:, :] = gram[THIN * j : THIN * (j + 1), :]
    turned[...] = jnp.concatenate(two_terms(tall[...]), axis=1).T
    for n in range(X):
        for ref, side in sides:
            columns = pl.ds(pl.multiple_of(side * HALF + Y * WIDE * n, Y * WIDE), Y * WIDE)
            both = quick_dot(turned[...], held[:, columns])
            terms = both[:K] + both[K:]
            for i in range(Y):
                ref[slot(side, n, i), :K, :] = terms[:, WIDE * i : WIDE * (i + 1)]


def start_kernel(core, x, y, data, sketch, first, give, keep, held, turned, arrived):
    copies = fetch(data, held, arrived)
    for b in range(STEPS):
        copies[b].wait()
        rows = pl.ds(b * BLOCK, BLOCK)
        first[rows, :] = quick_dot(held[rows, :], sketch[...])
    make_message((core[0], x[0], y[0]), held, first, give, keep, turned)


def factor_kernel(own, inverse):
    inverse[...] = inverse_factor(jnp.concatenate([own[j, K:, :] for j in range(PLANE)], axis=0))


def middle_kernel(core, x, y, own, other, inverse, held, second, give, keep, back, turned):
    scaled = inverse[...] * (1.0 / ROOT_ROWS)

    def store(start, terms):
        back[:, pl.ds(start, 2 * WIDE)] = terms.astype(jnp.bfloat16)

    apply_everywhere(core[0], own, other, scaled, store)
    for b in range(STEPS):
        rows = pl.ds(b * BLOCK, BLOCK)
        second[rows, :] = quick_dot(held[rows, :], back[...], ((1,), (1,)))
    make_message((core[0], x[0], y[0]), held, second, give, keep, turned)


def final_kernel(core, x, y, own, other, inverse, tall, projected, basis, wide, narrow, sent):
    scaled = inverse[...] * (D**0.5 / ROOT_ROWS)

    def store(start, terms):
        wide[:, pl.ds(start, 2 * WIDE)] = terms

    apply_everywhere(core[0], own, other, scaled, store)
    one = pltpu.make_async_copy(wide, projected, sent.at[0])
    one.start()
    narrow[...] = exact_dot(tall[...], inverse[...] * ROOT_ROWS, ((1,), (1,)))
    two = pltpu.make_async_copy(narrow, basis, sent.at[1])
    two.start()
    one.wait()
    two.wait()


def params(mebibytes=32):
    return pltpu.CompilerParams(vmem_limit_bytes=mebibytes * 2**20)


VM = pl.BlockSpec(memory_space=pltpu.VMEM)
SM = pl.BlockSpec(memory_space=pltpu.SMEM)
ANY = pl.BlockSpec(memory_space=pl.ANY)
MESSAGE = jax.ShapeDtypeStruct((PLANE, ROWS, K), jnp.float32)
SQUARE = jax.ShapeDtypeStruct((K, K), jnp.float32)


def start_call(place, data, sketch):
    rows = data.shape[0]
    return pl.pallas_call(
        start_kernel,
        out_shape=(jax.ShapeDtypeStruct((rows, K), jnp.float32), MESSAGE, MESSAGE),
        in_specs=[SM, SM, SM, ANY, VM],
        out_specs=(VM, VM, VM),
        scratch_shapes=[
            pltpu.VMEM(data.shape, jnp.bfloat16),
            pltpu.VMEM((2 * K, rows), jnp.bfloat16),
            pltpu.SemaphoreType.DMA((STEPS,)),
        ],
        compiler_params=params(48),
        name="start",
    )(*place, data, sketch)


def factor_call(own):
    return pl.pallas_call(
        factor_kernel,
        out_shape=SQUARE,
        in_specs=[VM],
        out_specs=VM,
        compiler_params=params(),
        cost_estimate=pl.CostEstimate(flops=K**3, bytes_accessed=10**6, transcendentals=0),
        name="factor",
    )(own)


def middle_call(place, own, other, inverse, held):
    rows = held.shape[0]
    return pl.pallas_call(
        middle_kernel,
        out_shape=(jax.ShapeDtypeStruct((rows, K), jnp.float32), MESSAGE, MESSAGE),
        in_specs=[SM, SM, SM, VM, VM, VM, VM],
        out_specs=(VM, VM, VM),
        scratch_shapes=[pltpu.VMEM((K, D), jnp.bfloat16), pltpu.VMEM((2 * K, rows), jnp.bfloat16)],
        compiler_params=params(),
        name="middle",
    )(*place, own, other, inverse, held)


def final_call(place, own, other, inverse, tall):
    return pl.pallas_call(
        final_kernel,
        out_shape=(jax.ShapeDtypeStruct((K, D), jnp.float32), jax.ShapeDtypeStruct(tall.shape, jnp.float32)),
        in_specs=[SM, SM, SM, VM, VM, VM, VM],
        out_specs=(ANY, ANY),
        scratch_shapes=[
            pltpu.VMEM((K, D), jnp.float32),
            pltpu.VMEM(tall.shape, jnp.float32),
            pltpu.SemaphoreType.DMA((2,)),
        ],
        compiler_params=params(),
        name="final",
    )(*place, own, other, inverse, tall)


def on_device(data, sketch):
    place = [lax.axis_index(axis).astype(jnp.int32).reshape(1) for axis in ("core", "x", "y")]
    first, give, keep = start_call(place, data, sketch)
    own, other, _ = sum_everywhere(give, keep)
    inverse = factor_call(own)
    second, give, keep = middle_call(place, own, other, inverse, data)
    first_basis = exact_dot(first, ROOT_ROWS * inverse, ((1,), (1,)))
    own, other, first_basis = sum_everywhere(give, keep, first_basis)
    inverse = factor_call(own)
    projected, basis = final_call(place, own, other, inverse, second)
    return (first_basis, basis, projected)


def solution(mesh):
    split = Mesh(mesh.devices.reshape(Z, X, C, Y), AXES)
    return jax.shard_map(
        on_device,
        mesh=split,
        in_specs=(P(AXES, None), P()),
        out_specs=(P(AXES, None), P(AXES, None), P()),
        check_vma=False,
    )
```

```python
import jax
import jax.numpy as jnp
from jax import lax
from jax.experimental import pallas as pl
from jax.experimental.pallas import tpu as pltpu
from jax.sharding import Mesh, PartitionSpec as P

D = 4096
K = 128
Z, X, C, Y = 8, 4, 2, 4
AXES = ("z", "x", "core", "y")
PLANE = X * Y
HALF = D // C
WIDE = HALF // PLANE
THIN = K // PLANE
ROWS = K + THIN
ROOT_ROWS = 512.0
BLOCK = 256
STEPS = 4


def device_number(z, x, core, y):
    return ((z * X + x) * C + core) * Y + y


def exchange(value, partner):
    pairs = []
    for z in range(Z):
        for x in range(X):
            for core in range(C):
                for y in range(Y):
                    pairs.append((device_number(z, x, core, y), device_number(*partner(z, x, core, y))))
    return lax.ppermute(value, AXES, pairs)


def other_core(value):
    return exchange(value, lambda z, x, core, y: (z, x, 1 - core, y))


def plane_partner(mask, first):
    def partner(z, x, core, y):
        return (z, x, core, y ^ mask) if (core == 0) == first else (z, x ^ mask, core, y)

    return partner


def column_partner(mask):
    def partner(z, x, core, y):
        return z ^ mask, x, core, y

    return partner


def sum_everywhere(give, keep, beside=()):
    far, near = [mine + other_core(theirs) for mine, theirs in zip(keep, give)]
    arrived = [exchange(part, plane_partner(mask, True)) for part, mask in ((far[4:], 3), (near[4:], 1), (far[:4], 2))]
    half = near[:4] + arrived[0] + arrived[1] + arrived[2]
    arrived = [exchange(half[mask], plane_partner(mask, False)) for mask in (2, 1, 3)]
    part = half[0] + arrived[0] + arrived[1] + arrived[2]
    arrived = [exchange(part, column_partner(mask)) for mask in (3, 2, 1)]
    arrived, beside = lax.optimization_barrier((arrived, beside))
    part = part + arrived[0] + arrived[1] + arrived[2]
    part = part + exchange(part, column_partner(6))
    own = lax.all_to_all(
        jnp.broadcast_to(part, (PLANE,) + part.shape), ("x", "y"), split_axis=0, concat_axis=0, tiled=True
    )
    return own, other_core(own), beside


def exact_dot(left, right, dims):
    return lax.dot_general(
        left, right, (dims, ((), ())), precision=lax.Precision.HIGHEST, preferred_element_type=jnp.float32
    )


def quick_dot(left, right, dims=((1,), (0,))):
    return lax.dot_general(left, right, (dims, ((), ())), preferred_element_type=jnp.float32)


def two_terms(value):
    high = value.astype(jnp.bfloat16)
    return high, (value - high.astype(jnp.float32)).astype(jnp.bfloat16)


def reciprocal(value):
    rough = pl.reciprocal(value, approx=True)
    return rough * (2.0 - value * rough)


def inverse_factor(gram):
    row = lax.broadcasted_iota(jnp.int32, (K, K), 0)
    column = lax.broadcasted_iota(jnp.int32, (K, K), 1)
    diagonal = jnp.where(row == column, gram, 0.0)
    across = lax.rsqrt(jnp.sum(diagonal, axis=0, keepdims=True))
    down = lax.rsqrt(jnp.sum(diagonal, axis=1, keepdims=True))
    scaled = gram * across * down
    groups = [scaled[8 * g : 8 * g + 8] for g in range(K // 8)]
    lane = lax.broadcasted_iota(jnp.int32, (8, K), 1)
    sub = lax.broadcasted_iota(jnp.int32, (8, K), 0)

    def spread(value, k):
        return jnp.broadcast_to(value[:, k : k + 1], (8, K))

    for g0 in range(K // 8):
        k = 8 * g0
        mine = groups[g0]
        columns = [spread(mine, k + t) for t in range(8)]
        s = {(i, j): jnp.broadcast_to(columns[j][i : i + 1], (8, K)) for i in range(8) for j in range(i + 1)}
        inside = (lane >= k) & (lane < k + 8)
        e = [
            jnp.where(inside, jnp.where(lane == k + t, 1.0, 0.0), jnp.broadcast_to(mine[t : t + 1], (8, K)))
            for t in range(8)
        ]
        u, v, done = [None] * 8, {}, [None] * 8
        for h in (0, 2, 4, 6):
            a, b, c = s[h, h], s[h + 1, h], s[h + 1, h + 1]
            turn = reciprocal(a * c - b * b)
            n0, n1 = c * e[h] - b * e[h + 1], a * e[h + 1] - b * e[h]
            root = lax.rsqrt(a)
            ratio = b * (root * root)
            done[h] = e[h] * root
            done[h + 1] = (e[h + 1] - ratio * e[h]) * lax.rsqrt(c - ratio * b)
            u[h], u[h + 1] = n0 * turn, n1 * turn
            m = {}
            for i in range(h + 2, 8):
                m[i] = (c * s[i, h] - b * s[i, h + 1], a * s[i, h + 1] - b * s[i, h])
                v[i, h] = (m[i][0] * turn, m[i][1] * turn)
                e[i] = e[i] - (s[i, h] * n0 + s[i, h + 1] * n1) * turn
                for j in range(h + 2, i + 1):
                    s[i, j] = s[i, j] - (s[i, h] * m[j][0] + s[i, h + 1] * m[j][1]) * turn
        for h in (4, 2, 0):
            for i in range(h + 2, 8):
                u[h] = u[h] - v[i, h][0] * u[i]
                u[h + 1] = u[h + 1] - v[i, h][1] * u[i]
        for g in range(g0 + 1, K // 8):
            value = jnp.where(inside, 0.0, groups[g])
            for t in (6, 4, 2, 0):
                value = value - (spread(groups[g], k + t) * u[t] + spread(groups[g], k + t + 1) * u[t + 1])
            groups[g] = value
        value = done[0]
        for t in range(1, 8):
            value = jnp.where(sub == t, done[t], value)
        groups[g0] = value
    full = jnp.concatenate(groups, axis=0)
    return jnp.where(row >= column, full, 0.0) * across


def three_term_gram(block):
    high, low = two_terms(block)
    rest = (block - high.astype(jnp.float32) - low.astype(jnp.float32)).astype(jnp.bfloat16)
    both = jnp.concatenate([high, low], axis=1)
    main = quick_dot(both, both, ((0,), (0,)))
    side = quick_dot(high, rest, ((0,), (0,)))
    return main[:K, :K] + (main[:K, K:] + main[K:, :K]) + (main[K:, K:] + side + side.T)


def apply_factor(inverse, terms):
    high, low = two_terms(inverse)
    left = jnp.concatenate(
        [jnp.concatenate([high, high], axis=1), jnp.concatenate([low, jnp.zeros_like(low)], axis=1)], axis=0
    )
    both = quick_dot(left, jnp.concatenate(two_terms(terms), axis=0))
    return both[:K] + both[K:]


def place_of(chunk, side):
    return jnp.where(side == 0, Y * (chunk % X) + chunk // X, chunk)


def apply_everywhere(core, own, other, inverse, store):
    for n in range(PLANE // 2):
        for ref, side in ((own, core), (other, 1 - core)):
            pair = [ref[place_of(2 * n + i, side), :K, :] for i in (0, 1)]
            store(
                pl.multiple_of(side * HALF + 2 * WIDE * n, 2 * WIDE),
                apply_factor(inverse, jnp.concatenate(pair, axis=1)),
            )


def fetch(data, held, arrived):
    copies = [
        pltpu.make_async_copy(data.at[pl.ds(b * BLOCK, BLOCK)], held.at[pl.ds(b * BLOCK, BLOCK)], arrived.at[b])
        for b in range(STEPS)
    ]
    for copy in copies:
        copy.start()
    return copies


def make_message(place, held, tall, give, keep, turned, gram):
    core, x, y = place
    gram[...] = three_term_gram(tall[...])
    turned[...] = jnp.concatenate(two_terms(tall[...]), axis=1).T
    for a in (2, 3, 0, 1):
        for refs, side in ((give, 1 - core), (keep, core)):
            ref = refs[0] if a >= 2 else refs[1]
            p = a ^ jnp.where(side == 0, y, x)
            q = jnp.where(side == 0, x, y)
            columns = pl.ds(pl.multiple_of(side * HALF + 4 * WIDE * p, 4 * WIDE), 4 * WIDE)
            both = quick_dot(turned[...], held[:, columns])
            terms = both[:K] + both[K:]
            for i in range(4):
                slot = 4 * (a % 2) + (i ^ q)
                ref[slot, :K, :] = terms[:, WIDE * i : WIDE * (i + 1)]
                ref[slot, K:, :] = gram[pl.ds(pl.multiple_of(THIN * (4 * p + i), THIN), THIN), :]


def start_kernel(core, x, y, data, sketch, first, give2, give0, keep2, keep0, held, turned, gram, arrived):
    copies = fetch(data, held, arrived)
    for b in range(STEPS):
        copies[b].wait()
        rows = pl.ds(b * BLOCK, BLOCK)
        first[rows, :] = quick_dot(held[rows, :], sketch[...])
    make_message((core[0], x[0], y[0]), held, first, (give2, give0), (keep2, keep0), turned, gram)


def factor_kernel(core, own, inverse):
    rows = [own[place_of(chunk, core[0]), K:, :] for chunk in range(PLANE)]
    inverse[...] = inverse_factor(jnp.concatenate(rows, axis=0))


def middle_kernel(core, x, y, own, other, inverse, held, second, give2, give0, keep2, keep0, back, turned, gram):
    scaled = inverse[...] * (1.0 / ROOT_ROWS)

    def store(start, terms):
        back[:, pl.ds(start, 2 * WIDE)] = terms.astype(jnp.bfloat16)

    apply_everywhere(core[0], own, other, scaled, store)
    for b in range(STEPS):
        rows = pl.ds(b * BLOCK, BLOCK)
        second[rows, :] = quick_dot(held[rows, :], back[...], ((1,), (1,)))
    make_message((core[0], x[0], y[0]), held, second, (give2, give0), (keep2, keep0), turned, gram)


def final_kernel(core, x, y, own, other, inverse, tall, projected, basis, wide, narrow, sent):
    scaled = inverse[...] * (D**0.5 / ROOT_ROWS)

    def store(start, terms):
        wide[:, pl.ds(start, 2 * WIDE)] = terms

    apply_everywhere(core[0], own, other, scaled, store)
    one = pltpu.make_async_copy(wide, projected, sent.at[0])
    one.start()
    narrow[...] = exact_dot(tall[...], inverse[...] * ROOT_ROWS, ((1,), (1,)))
    two = pltpu.make_async_copy(narrow, basis, sent.at[1])
    two.start()
    one.wait()
    two.wait()


def params(mebibytes=32):
    return pltpu.CompilerParams(vmem_limit_bytes=mebibytes * 2**20)


VM = pl.BlockSpec(memory_space=pltpu.VMEM)
SM = pl.BlockSpec(memory_space=pltpu.SMEM)
ANY = pl.BlockSpec(memory_space=pl.ANY)
PART = jax.ShapeDtypeStruct((PLANE // 2, ROWS, K), jnp.float32)
SQUARE = jax.ShapeDtypeStruct((K, K), jnp.float32)


def start_call(place, data, sketch):
    rows = data.shape[0]
    return pl.pallas_call(
        start_kernel,
        out_shape=(jax.ShapeDtypeStruct((rows, K), jnp.float32), PART, PART, PART, PART),
        in_specs=[SM, SM, SM, ANY, VM],
        out_specs=(VM,) * 5,
        scratch_shapes=[
            pltpu.VMEM(data.shape, jnp.bfloat16),
            pltpu.VMEM((2 * K, rows), jnp.bfloat16),
            pltpu.VMEM((K, K), jnp.float32),
            pltpu.SemaphoreType.DMA((STEPS,)),
        ],
        compiler_params=params(48),
        name="start",
    )(*place, data, sketch)


def factor_call(core, own):
    return pl.pallas_call(
        factor_kernel,
        out_shape=SQUARE,
        in_specs=[SM, VM],
        out_specs=VM,
        compiler_params=params(),
        cost_estimate=pl.CostEstimate(flops=K**3, bytes_accessed=10**6, transcendentals=0),
        name="factor",
    )(core, own)


def middle_call(place, own, other, inverse, held):
    rows = held.shape[0]
    return pl.pallas_call(
        middle_kernel,
        out_shape=(jax.ShapeDtypeStruct((rows, K), jnp.float32), PART, PART, PART, PART),
        in_specs=[SM, SM, SM, VM, VM, VM, VM],
        out_specs=(VM,) * 5,
        scratch_shapes=[
            pltpu.VMEM((K, D), jnp.bfloat16),
            pltpu.VMEM((2 * K, rows), jnp.bfloat16),
            pltpu.VMEM((K, K), jnp.float32),
        ],
        compiler_params=params(),
        name="middle",
    )(*place, own, other, inverse, held)


def final_call(place, own, other, inverse, tall):
    return pl.pallas_call(
        final_kernel,
        out_shape=(jax.ShapeDtypeStruct((K, D), jnp.float32), jax.ShapeDtypeStruct(tall.shape, jnp.float32)),
        in_specs=[SM, SM, SM, VM, VM, VM, VM],
        out_specs=(ANY, ANY),
        scratch_shapes=[
            pltpu.VMEM((K, D), jnp.float32),
            pltpu.VMEM(tall.shape, jnp.float32),
            pltpu.SemaphoreType.DMA((2,)),
        ],
        compiler_params=params(),
        name="final",
    )(*place, own, other, inverse, tall)


def on_device(data, sketch):
    place = [lax.axis_index(axis).astype(jnp.int32).reshape(1) for axis in ("core", "x", "y")]
    first, *parts = start_call(place, data, sketch)
    own, other, _ = sum_everywhere(parts[:2], parts[2:])
    inverse = factor_call(place[0], own)
    second, *parts = middle_call(place, own, other, inverse, data)
    first_basis = exact_dot(first, ROOT_ROWS * inverse, ((1,), (1,)))
    own, other, first_basis = sum_everywhere(parts[:2], parts[2:], first_basis)
    inverse = factor_call(place[0], own)
    projected, basis = final_call(place, own, other, inverse, second)
    return (first_basis, basis, projected)


def solution(mesh):
    split = Mesh(mesh.devices.reshape(Z, X, C, Y), AXES)
    return jax.shard_map(
        on_device,
        mesh=split,
        in_specs=(P(AXES, None), P()),
        out_specs=(P(AXES, None), P(AXES, None), P()),
        check_vma=False,
    )
```

```python
import jax
import jax.numpy as jnp
from jax import lax
from jax.experimental import pallas as pl
from jax.experimental.pallas import tpu as pltpu
from jax.sharding import Mesh, PartitionSpec as P

D = 4096
K = 128
Z, X, C, Y = 8, 4, 2, 4
AXES = ("z", "x", "core", "y")
PLANE = X * Y
HALF = D // C
WIDE = HALF // PLANE
THIN = K // PLANE
ROWS = K + THIN
ROOT_ROWS = 512.0
BLOCK = 256
STEPS = 4


def device_number(z, x, core, y):
    return ((z * X + x) * C + core) * Y + y


def exchange(value, partner):
    pairs = []
    for z in range(Z):
        for x in range(X):
            for core in range(C):
                for y in range(Y):
                    pairs.append((device_number(z, x, core, y), device_number(*partner(z, x, core, y))))
    return lax.ppermute(value, AXES, pairs)


def other_core(value):
    return exchange(value, lambda z, x, core, y: (z, x, 1 - core, y))


def plane_partner(mask, first):
    def partner(z, x, core, y):
        return (z, x, core, y ^ mask) if (core == 0) == first else (z, x ^ mask, core, y)

    return partner


def column_partner(mask):
    def partner(z, x, core, y):
        return z ^ mask, x, core, y

    return partner


def sum_everywhere(give, keep, beside=()):
    far, near = [mine + other_core(theirs) for mine, theirs in zip(keep, give)]
    arrived = [exchange(part, plane_partner(mask, True)) for part, mask in ((far[4:], 3), (near[4:], 1), (far[:4], 2))]
    half = near[:4] + arrived[0] + arrived[1] + arrived[2]
    arrived = [exchange(half[mask], plane_partner(mask, False)) for mask in (2, 1, 3)]
    part = half[0] + arrived[0] + arrived[1] + arrived[2]
    arrived = [exchange(part, column_partner(mask)) for mask in (3, 2, 1)]
    arrived, beside = lax.optimization_barrier((arrived, beside))
    part = part + arrived[0] + arrived[1] + arrived[2]
    part = part + exchange(part, column_partner(6))
    own = lax.all_to_all(
        jnp.broadcast_to(part, (PLANE,) + part.shape), ("x", "y"), split_axis=0, concat_axis=0, tiled=True
    )
    return own, other_core(own), beside


def exact_dot(left, right, dims):
    return lax.dot_general(
        left, right, (dims, ((), ())), precision=lax.Precision.HIGHEST, preferred_element_type=jnp.float32
    )


def quick_dot(left, right, dims=((1,), (0,))):
    return lax.dot_general(left, right, (dims, ((), ())), preferred_element_type=jnp.float32)


def two_terms(value):
    high = value.astype(jnp.bfloat16)
    return high, (value - high.astype(jnp.float32)).astype(jnp.bfloat16)


def reciprocal(value):
    rough = pl.reciprocal(value, approx=True)
    return rough * (2.0 - value * rough)


def inverse_factor(gram, panel, spreads):
    row = lax.broadcasted_iota(jnp.int32, (K, K), 0)
    column = lax.broadcasted_iota(jnp.int32, (K, K), 1)
    diagonal = jnp.where(row == column, gram, 0.0)
    across = lax.rsqrt(jnp.sum(diagonal, axis=0, keepdims=True))
    down = lax.rsqrt(jnp.sum(diagonal, axis=1, keepdims=True))
    scaled = gram * across * down
    groups = [scaled[8 * g : 8 * g + 8] for g in range(K // 8)]
    lane = lax.broadcasted_iota(jnp.int32, (8, K), 1)
    sub = lax.broadcasted_iota(jnp.int32, (8, K), 0)

    def spread(value, k):
        return jnp.broadcast_to(value[:, k : k + 1], (8, K))

    for g0 in range(K // 8):
        k = 8 * g0
        mine = groups[g0]
        columns = [spread(mine, k + t) for t in range(8)]
        panel[...] = mine
        for j in range(8):
            spreads[8 * j : 8 * j + 8, :] = columns[j]
        s = {
            (i, j): jnp.broadcast_to(spreads[8 * j + i : 8 * j + i + 1, :], (8, K))
            for i in range(8)
            for j in range(i + 1)
        }
        inside = (lane >= k) & (lane < k + 8)
        e = [
            jnp.where(inside, jnp.where(lane == k + t, 1.0, 0.0), jnp.broadcast_to(panel[t : t + 1, :], (8, K)))
            for t in range(8)
        ]
        u, v, done = [None] * 8, {}, [None] * 8
        for h in (0, 2, 4, 6):
            a, b, c = s[h, h], s[h + 1, h], s[h + 1, h + 1]
            turn = reciprocal(a * c - b * b)
            n0, n1 = c * e[h] - b * e[h + 1], a * e[h + 1] - b * e[h]
            root = lax.rsqrt(a)
            ratio = b * (root * root)
            done[h] = e[h] * root
            done[h + 1] = (e[h + 1] - ratio * e[h]) * lax.rsqrt(c - ratio * b)
            u[h], u[h + 1] = n0 * turn, n1 * turn
            m = {}
            for i in range(h + 2, 8):
                m[i] = (c * s[i, h] - b * s[i, h + 1], a * s[i, h + 1] - b * s[i, h])
                v[i, h] = (m[i][0] * turn, m[i][1] * turn)
                e[i] = e[i] - (s[i, h] * n0 + s[i, h + 1] * n1) * turn
                for j in range(h + 2, i + 1):
                    s[i, j] = s[i, j] - (s[i, h] * m[j][0] + s[i, h + 1] * m[j][1]) * turn
        for h in (4, 2, 0):
            for i in range(h + 2, 8):
                u[h] = u[h] - v[i, h][0] * u[i]
                u[h + 1] = u[h + 1] - v[i, h][1] * u[i]
        for g in range(g0 + 1, K // 8):
            value = jnp.where(inside, 0.0, groups[g])
            for t in (6, 4, 2, 0):
                value = value - (spread(groups[g], k + t) * u[t] + spread(groups[g], k + t + 1) * u[t + 1])
            groups[g] = value
        value = done[0]
        for t in range(1, 8):
            value = jnp.where(sub == t, done[t], value)
        groups[g0] = value
    full = jnp.concatenate(groups, axis=0)
    return jnp.where(row >= column, full, 0.0) * across


def three_term_gram(block):
    high, low = two_terms(block)
    rest = (block - high.astype(jnp.float32) - low.astype(jnp.float32)).astype(jnp.bfloat16)
    both = jnp.concatenate([high, low], axis=1)
    main = quick_dot(both, both, ((0,), (0,)))
    side = quick_dot(high, rest, ((0,), (0,)))
    return main[:K, :K] + (main[:K, K:] + main[K:, :K]) + (main[K:, K:] + side + side.T)


def apply_factor(inverse, terms):
    high, low = two_terms(inverse)
    left = jnp.concatenate(
        [jnp.concatenate([high, high], axis=1), jnp.concatenate([low, jnp.zeros_like(low)], axis=1)], axis=0
    )
    both = quick_dot(left, jnp.concatenate(two_terms(terms), axis=0))
    return both[:K] + both[K:]


def place_of(chunk, side):
    return jnp.where(side == 0, Y * (chunk % X) + chunk // X, chunk)


def apply_everywhere(core, own, other, inverse, store):
    for n in range(PLANE // 2):
        for ref, side in ((own, core), (other, 1 - core)):
            pair = [ref[place_of(2 * n + i, side), :K, :] for i in (0, 1)]
            store(
                pl.multiple_of(side * HALF + 2 * WIDE * n, 2 * WIDE),
                apply_factor(inverse, jnp.concatenate(pair, axis=1)),
            )


def fetch(data, held, arrived):
    copies = [
        pltpu.make_async_copy(data.at[pl.ds(b * BLOCK, BLOCK)], held.at[pl.ds(b * BLOCK, BLOCK)], arrived.at[b])
        for b in range(STEPS)
    ]
    for copy in copies:
        copy.start()
    return copies


def prepare(tall, turned, gram):
    gram[...] = three_term_gram(tall[...])
    turned[...] = jnp.concatenate(two_terms(tall[...]), axis=1).T


def make_message(place, held, turned, gram, give, keep):
    core, x, y = place
    for a in (2, 3, 0, 1):
        for refs, side in ((give, 1 - core), (keep, core)):
            if refs is None:
                continue
            ref = refs[0] if a >= 2 else refs[1]
            p = a ^ jnp.where(side == 0, y, x)
            q = jnp.where(side == 0, x, y)
            columns = pl.ds(pl.multiple_of(side * HALF + 4 * WIDE * p, 4 * WIDE), 4 * WIDE)
            both = quick_dot(turned[...], held[:, columns])
            terms = both[:K] + both[K:]
            for i in range(4):
                slot = 4 * (a % 2) + (i ^ q)
                ref[slot, :K, :] = terms[:, WIDE * i : WIDE * (i + 1)]
                ref[slot, K:, :] = gram[pl.ds(pl.multiple_of(THIN * (4 * p + i), THIN), THIN), :]


def start_kernel(core, x, y, data, sketch, first, give2, give0, keep2, keep0, held, turned, gram, arrived):
    copies = fetch(data, held, arrived)
    for b in range(STEPS):
        copies[b].wait()
        rows = pl.ds(b * BLOCK, BLOCK)
        first[rows, :] = quick_dot(held[rows, :], sketch[...])
    prepare(first, turned, gram)
    make_message((core[0], x[0], y[0]), held, turned, gram, (give2, give0), (keep2, keep0))


def factor_kernel(core, own, inverse, panel, spreads):
    rows = [own[place_of(chunk, core[0]), K:, :] for chunk in range(PLANE)]
    inverse[...] = inverse_factor(jnp.concatenate(rows, axis=0), panel, spreads)


def middle_kernel(core, x, y, own, other, inverse, held, second, turned, gram, give2, give0, back):
    scaled = inverse[...] * (1.0 / ROOT_ROWS)

    def store(start, terms):
        back[:, pl.ds(start, 2 * WIDE)] = terms.astype(jnp.bfloat16)

    apply_everywhere(core[0], own, other, scaled, store)
    for b in range(STEPS):
        rows = pl.ds(b * BLOCK, BLOCK)
        second[rows, :] = quick_dot(held[rows, :], back[...], ((1,), (1,)))
    prepare(second, turned, gram)
    make_message((core[0], x[0], y[0]), held, turned, gram, (give2, give0), None)


def keep_kernel(core, x, y, held, turned, gram, keep2, keep0):
    make_message((core[0], x[0], y[0]), held, turned, gram, None, (keep2, keep0))


def final_kernel(core, x, y, own, other, inverse, tall, projected, basis, wide, narrow, sent):
    scaled = inverse[...] * (D**0.5 / ROOT_ROWS)

    def store(start, terms):
        wide[:, pl.ds(start, 2 * WIDE)] = terms

    apply_everywhere(core[0], own, other, scaled, store)
    one = pltpu.make_async_copy(wide, projected, sent.at[0])
    one.start()
    narrow[...] = exact_dot(tall[...], inverse[...] * ROOT_ROWS, ((1,), (1,)))
    two = pltpu.make_async_copy(narrow, basis, sent.at[1])
    two.start()
    one.wait()
    two.wait()


def params(mebibytes=32):
    return pltpu.CompilerParams(vmem_limit_bytes=mebibytes * 2**20)


VM = pl.BlockSpec(memory_space=pltpu.VMEM)
SM = pl.BlockSpec(memory_space=pltpu.SMEM)
ANY = pl.BlockSpec(memory_space=pl.ANY)
PART = jax.ShapeDtypeStruct((PLANE // 2, ROWS, K), jnp.float32)
SQUARE = jax.ShapeDtypeStruct((K, K), jnp.float32)


def start_call(place, data, sketch):
    rows = data.shape[0]
    return pl.pallas_call(
        start_kernel,
        out_shape=(jax.ShapeDtypeStruct((rows, K), jnp.float32), PART, PART, PART, PART),
        in_specs=[SM, SM, SM, ANY, VM],
        out_specs=(VM,) * 5,
        scratch_shapes=[
            pltpu.VMEM(data.shape, jnp.bfloat16),
            pltpu.VMEM((2 * K, rows), jnp.bfloat16),
            pltpu.VMEM((K, K), jnp.float32),
            pltpu.SemaphoreType.DMA((STEPS,)),
        ],
        compiler_params=params(48),
        name="start",
    )(*place, data, sketch)


def factor_call(core, own):
    return pl.pallas_call(
        factor_kernel,
        out_shape=SQUARE,
        in_specs=[SM, VM],
        out_specs=VM,
        scratch_shapes=[pltpu.VMEM((8, K), jnp.float32), pltpu.VMEM((64, K), jnp.float32)],
        compiler_params=params(),
        cost_estimate=pl.CostEstimate(flops=K**3, bytes_accessed=10**6, transcendentals=0),
        name="factor",
    )(core, own)


def middle_call(place, own, other, inverse, held):
    rows = held.shape[0]
    return pl.pallas_call(
        middle_kernel,
        out_shape=(
            jax.ShapeDtypeStruct((rows, K), jnp.float32),
            jax.ShapeDtypeStruct((2 * K, rows), jnp.bfloat16),
            SQUARE,
            PART,
            PART,
        ),
        in_specs=[SM, SM, SM, VM, VM, VM, VM],
        out_specs=(VM,) * 5,
        scratch_shapes=[pltpu.VMEM((K, D), jnp.bfloat16)],
        compiler_params=params(),
        name="middle",
    )(*place, own, other, inverse, held)


def keep_call(place, held, turned, gram):
    return pl.pallas_call(
        keep_kernel,
        out_shape=(PART, PART),
        in_specs=[SM, SM, SM, VM, VM, VM],
        out_specs=(VM, VM),
        compiler_params=params(),
        cost_estimate=pl.CostEstimate(flops=2 * K * held.size, bytes_accessed=10**6, transcendentals=0),
        name="keep",
    )(*place, held, turned, gram)


def final_call(place, own, other, inverse, tall):
    return pl.pallas_call(
        final_kernel,
        out_shape=(jax.ShapeDtypeStruct((K, D), jnp.float32), jax.ShapeDtypeStruct(tall.shape, jnp.float32)),
        in_specs=[SM, SM, SM, VM, VM, VM, VM],
        out_specs=(ANY, ANY),
        scratch_shapes=[
            pltpu.VMEM((K, D), jnp.float32),
            pltpu.VMEM(tall.shape, jnp.float32),
            pltpu.SemaphoreType.DMA((2,)),
        ],
        compiler_params=params(),
        name="final",
    )(*place, own, other, inverse, tall)


def on_device(data, sketch):
    place = [lax.axis_index(axis).astype(jnp.int32).reshape(1) for axis in ("core", "x", "y")]
    first, *parts = start_call(place, data, sketch)
    own, other, _ = sum_everywhere(parts[:2], parts[2:])
    inverse = factor_call(place[0], own)
    second, turned, gram, *give = middle_call(place, own, other, inverse, data)
    keep = keep_call(place, data, turned, gram)
    first_basis = exact_dot(first, ROOT_ROWS * inverse, ((1,), (1,)))
    own, other, first_basis = sum_everywhere(give, keep, first_basis)
    inverse = factor_call(place[0], own)
    projected, basis = final_call(place, own, other, inverse, second)
    return (first_basis, basis, projected)


def solution(mesh):
    split = Mesh(mesh.devices.reshape(Z, X, C, Y), AXES)
    return jax.shard_map(
        on_device,
        mesh=split,
        in_specs=(P(AXES, None), P()),
        out_specs=(P(AXES, None), P(AXES, None), P()),
        check_vma=False,
    )
```

```python
import jax
import jax.numpy as jnp
from jax import lax
from jax.experimental import pallas as pl
from jax.experimental.pallas import tpu as pltpu
from jax.sharding import Mesh, PartitionSpec as P

D = 4096
K = 128
Z, X, C, Y = 8, 4, 2, 4
AXES = ("z", "x", "core", "y")
PLANE = X * Y
HALF = D // C
WIDE = HALF // PLANE
THIN = K // PLANE
ROWS = K + THIN
ROOT_ROWS = 512.0
BLOCK = 256
STEPS = 4


def device_number(z, x, core, y):
    return ((z * X + x) * C + core) * Y + y


def exchange(value, partner):
    pairs = []
    for z in range(Z):
        for x in range(X):
            for core in range(C):
                for y in range(Y):
                    pairs.append((device_number(z, x, core, y), device_number(*partner(z, x, core, y))))
    return lax.ppermute(value, AXES, pairs)


def other_core(value):
    return exchange(value, lambda z, x, core, y: (z, x, 1 - core, y))


def plane_partner(mask, first):
    def partner(z, x, core, y):
        return (z, x, core, y ^ mask) if (core == 0) == first else (z, x ^ mask, core, y)

    return partner


def column_partner(mask):
    def partner(z, x, core, y):
        return z ^ mask, x, core, y

    return partner


def sum_everywhere(give, keep, beside=()):
    far, near = [[(mine[i : i + 4], other[i : i + 4]) for i in (0, 4)] for mine, other in zip(keep, map(other_core, give))]
    far, near = [[mine + other for mine, other in pair] for pair in (far, near)]
    arrived = [exchange(part, plane_partner(mask, True)) for part, mask in ((far[1], 3), (near[1], 1), (far[0], 2))]
    half = [near[0][b] + arrived[0][b] + arrived[1][b] + arrived[2][b] for b in range(4)]
    arrived = [exchange(half[mask], plane_partner(mask, False)) for mask in (2, 1, 3)]
    part = half[0] + arrived[0] + arrived[1] + arrived[2]
    arrived = [exchange(part, column_partner(mask)) for mask in (3, 2, 1)]
    arrived, beside = lax.optimization_barrier((arrived, beside))
    part = part + arrived[0] + arrived[1] + arrived[2]
    part = part + exchange(part, column_partner(6))
    own = lax.all_to_all(
        jnp.broadcast_to(part, (PLANE,) + part.shape), ("x", "y"), split_axis=0, concat_axis=0, tiled=True
    )
    return own, other_core(own), beside


def exact_dot(left, right, dims):
    return lax.dot_general(
        left, right, (dims, ((), ())), precision=lax.Precision.HIGHEST, preferred_element_type=jnp.float32
    )


def quick_dot(left, right, dims=((1,), (0,))):
    return lax.dot_general(left, right, (dims, ((), ())), preferred_element_type=jnp.float32)


def two_terms(value):
    high = value.astype(jnp.bfloat16)
    return high, (value - high.astype(jnp.float32)).astype(jnp.bfloat16)


def reciprocal(value):
    rough = pl.reciprocal(value, approx=True)
    return rough * (2.0 - value * rough)


def inverse_factor(gram, panel, spreads):
    row = lax.broadcasted_iota(jnp.int32, (K, K), 0)
    column = lax.broadcasted_iota(jnp.int32, (K, K), 1)
    diagonal = jnp.where(row == column, gram, 0.0)
    across = lax.rsqrt(jnp.sum(diagonal, axis=0, keepdims=True))
    down = lax.rsqrt(jnp.sum(diagonal, axis=1, keepdims=True))
    scaled = gram * across * down
    groups = [scaled[8 * g : 8 * g + 8] for g in range(K // 8)]
    lane = lax.broadcasted_iota(jnp.int32, (8, K), 1)
    sub = lax.broadcasted_iota(jnp.int32, (8, K), 0)

    def spread(value, k):
        return jnp.broadcast_to(value[:, k : k + 1], (8, K))

    for g0 in range(K // 8):
        k = 8 * g0
        mine = groups[g0]
        columns = [spread(mine, k + t) for t in range(8)]
        panel[...] = mine
        for j in range(8):
            spreads[8 * j : 8 * j + 8, :] = columns[j]
        s = {
            (i, j): jnp.broadcast_to(spreads[8 * j + i : 8 * j + i + 1, :], (8, K))
            for i in range(8)
            for j in range(i + 1)
        }
        inside = (lane >= k) & (lane < k + 8)
        e = [
            jnp.where(inside, jnp.where(lane == k + t, 1.0, 0.0), jnp.broadcast_to(panel[t : t + 1, :], (8, K)))
            for t in range(8)
        ]
        u, v, done = [None] * 8, {}, [None] * 8
        for h in (0, 2, 4, 6):
            a, b, c = s[h, h], s[h + 1, h], s[h + 1, h + 1]
            turn = reciprocal(a * c - b * b)
            n0, n1 = c * e[h] - b * e[h + 1], a * e[h + 1] - b * e[h]
            root = lax.rsqrt(a)
            ratio = b * (root * root)
            done[h] = e[h] * root
            done[h + 1] = (e[h + 1] - ratio * e[h]) * lax.rsqrt(c - ratio * b)
            u[h], u[h + 1] = n0 * turn, n1 * turn
            m = {}
            for i in range(h + 2, 8):
                m[i] = (c * s[i, h] - b * s[i, h + 1], a * s[i, h + 1] - b * s[i, h])
                v[i, h] = (m[i][0] * turn, m[i][1] * turn)
                e[i] = e[i] - (s[i, h] * n0 + s[i, h + 1] * n1) * turn
                for j in range(h + 2, i + 1):
                    s[i, j] = s[i, j] - (s[i, h] * m[j][0] + s[i, h + 1] * m[j][1]) * turn
        for h in (4, 2, 0):
            for i in range(h + 2, 8):
                u[h] = u[h] - v[i, h][0] * u[i]
                u[h + 1] = u[h + 1] - v[i, h][1] * u[i]
        for g in range(g0 + 1, K // 8):
            value = jnp.where(inside, 0.0, groups[g])
            for t in (6, 4, 2, 0):
                value = value - (spread(groups[g], k + t) * u[t] + spread(groups[g], k + t + 1) * u[t + 1])
            groups[g] = value
        value = done[0]
        for t in range(1, 8):
            value = jnp.where(sub == t, done[t], value)
        groups[g0] = value
    full = jnp.concatenate(groups, axis=0)
    return jnp.where(row >= column, full, 0.0) * across


def three_term_gram(block):
    high, low = two_terms(block)
    rest = (block - high.astype(jnp.float32) - low.astype(jnp.float32)).astype(jnp.bfloat16)
    both = jnp.concatenate([high, low], axis=1)
    main = quick_dot(both, both, ((0,), (0,)))
    side = quick_dot(high, rest, ((0,), (0,)))
    return main[:K, :K] + (main[:K, K:] + main[K:, :K]) + (main[K:, K:] + side + side.T)


def apply_factor(inverse, terms):
    high, low = two_terms(inverse)
    left = jnp.concatenate(
        [jnp.concatenate([high, high], axis=1), jnp.concatenate([low, jnp.zeros_like(low)], axis=1)], axis=0
    )
    both = quick_dot(left, jnp.concatenate(two_terms(terms), axis=0))
    return both[:K] + both[K:]


def place_of(chunk, side):
    return jnp.where(side == 0, Y * (chunk % X) + chunk // X, chunk)


def apply_everywhere(core, own, other, inverse, store):
    for n in range(PLANE // 2):
        for ref, side in ((own, core), (other, 1 - core)):
            pair = [ref[place_of(2 * n + i, side), :K, :] for i in (0, 1)]
            store(
                pl.multiple_of(side * HALF + 2 * WIDE * n, 2 * WIDE),
                apply_factor(inverse, jnp.concatenate(pair, axis=1)),
            )


def fetch(data, held, arrived):
    copies = [
        pltpu.make_async_copy(data.at[pl.ds(b * BLOCK, BLOCK)], held.at[pl.ds(b * BLOCK, BLOCK)], arrived.at[b])
        for b in range(STEPS)
    ]
    for copy in copies:
        copy.start()
    return copies


def prepare(tall, turned, gram):
    gram[...] = three_term_gram(tall[...])
    turned[...] = jnp.concatenate(two_terms(tall[...]), axis=1).T


def make_message(place, held, turned, gram, give, keep):
    core, x, y = place
    for a in (2, 3, 0, 1):
        for refs, side in ((give, 1 - core), (keep, core)):
            if refs is None:
                continue
            ref = refs[0] if a >= 2 else refs[1]
            p = a ^ jnp.where(side == 0, y, x)
            q = jnp.where(side == 0, x, y)
            columns = pl.ds(pl.multiple_of(side * HALF + 4 * WIDE * p, 4 * WIDE), 4 * WIDE)
            both = quick_dot(turned[...], held[:, columns])
            terms = both[:K] + both[K:]
            for i in range(4):
                slot = 4 * (a % 2) + (i ^ q)
                ref[slot, :K, :] = terms[:, WIDE * i : WIDE * (i + 1)]
                ref[slot, K:, :] = gram[pl.ds(pl.multiple_of(THIN * (4 * p + i), THIN), THIN), :]


def start_kernel(core, x, y, data, sketch, first, give2, give0, keep2, keep0, held, turned, gram, arrived):
    copies = fetch(data, held, arrived)
    for b in range(STEPS):
        copies[b].wait()
        rows = pl.ds(b * BLOCK, BLOCK)
        first[rows, :] = quick_dot(held[rows, :], sketch[...])
    prepare(first, turned, gram)
    make_message((core[0], x[0], y[0]), held, turned, gram, (give2, give0), (keep2, keep0))


def factor_kernel(core, own, inverse, panel, spreads):
    rows = [own[place_of(chunk, core[0]), K:, :] for chunk in range(PLANE)]
    inverse[...] = inverse_factor(jnp.concatenate(rows, axis=0), panel, spreads)


def middle_kernel(core, x, y, own, other, inverse, held, second, turned, gram, give2, give0, back):
    scaled = inverse[...] * (1.0 / ROOT_ROWS)

    def store(start, terms):
        back[:, pl.ds(start, 2 * WIDE)] = terms.astype(jnp.bfloat16)

    apply_everywhere(core[0], own, other, scaled, store)
    for b in range(STEPS):
        rows = pl.ds(b * BLOCK, BLOCK)
        second[rows, :] = quick_dot(held[rows, :], back[...], ((1,), (1,)))
    prepare(second, turned, gram)
    make_message((core[0], x[0], y[0]), held, turned, gram, (give2, give0), None)


def keep_kernel(core, x, y, held, turned, gram, keep2, keep0):
    make_message((core[0], x[0], y[0]), held, turned, gram, None, (keep2, keep0))


def final_kernel(core, x, y, own, other, inverse, tall, projected, basis, wide, narrow, sent):
    scaled = inverse[...] * (D**0.5 / ROOT_ROWS)

    def store(start, terms):
        wide[:, pl.ds(start, 2 * WIDE)] = terms

    apply_everywhere(core[0], own, other, scaled, store)
    one = pltpu.make_async_copy(wide, projected, sent.at[0])
    one.start()
    narrow[...] = exact_dot(tall[...], inverse[...] * ROOT_ROWS, ((1,), (1,)))
    two = pltpu.make_async_copy(narrow, basis, sent.at[1])
    two.start()
    one.wait()
    two.wait()


def params(mebibytes=32):
    return pltpu.CompilerParams(vmem_limit_bytes=mebibytes * 2**20)


VM = pl.BlockSpec(memory_space=pltpu.VMEM)
SM = pl.BlockSpec(memory_space=pltpu.SMEM)
ANY = pl.BlockSpec(memory_space=pl.ANY)
PART = jax.ShapeDtypeStruct((PLANE // 2, ROWS, K), jnp.float32)
SQUARE = jax.ShapeDtypeStruct((K, K), jnp.float32)


def start_call(place, data, sketch):
    rows = data.shape[0]
    return pl.pallas_call(
        start_kernel,
        out_shape=(jax.ShapeDtypeStruct((rows, K), jnp.float32), PART, PART, PART, PART),
        in_specs=[SM, SM, SM, ANY, VM],
        out_specs=(VM,) * 5,
        scratch_shapes=[
            pltpu.VMEM(data.shape, jnp.bfloat16),
            pltpu.VMEM((2 * K, rows), jnp.bfloat16),
            pltpu.VMEM((K, K), jnp.float32),
            pltpu.SemaphoreType.DMA((STEPS,)),
        ],
        compiler_params=params(48),
        name="start",
    )(*place, data, sketch)


def factor_call(core, own):
    return pl.pallas_call(
        factor_kernel,
        out_shape=SQUARE,
        in_specs=[SM, VM],
        out_specs=VM,
        scratch_shapes=[pltpu.VMEM((8, K), jnp.float32), pltpu.VMEM((64, K), jnp.float32)],
        compiler_params=params(),
        cost_estimate=pl.CostEstimate(flops=K**3, bytes_accessed=10**6, transcendentals=0),
        name="factor",
    )(core, own)


def middle_call(place, own, other, inverse, held):
    rows = held.shape[0]
    return pl.pallas_call(
        middle_kernel,
        out_shape=(
            jax.ShapeDtypeStruct((rows, K), jnp.float32),
            jax.ShapeDtypeStruct((2 * K, rows), jnp.bfloat16),
            SQUARE,
            PART,
            PART,
        ),
        in_specs=[SM, SM, SM, VM, VM, VM, VM],
        out_specs=(VM,) * 5,
        scratch_shapes=[pltpu.VMEM((K, D), jnp.bfloat16)],
        compiler_params=params(),
        name="middle",
    )(*place, own, other, inverse, held)


def keep_call(place, held, turned, gram):
    return pl.pallas_call(
        keep_kernel,
        out_shape=(PART, PART),
        in_specs=[SM, SM, SM, VM, VM, VM],
        out_specs=(VM, VM),
        compiler_params=params(),
        cost_estimate=pl.CostEstimate(flops=2 * K * held.size, bytes_accessed=10**6, transcendentals=0),
        name="keep",
    )(*place, held, turned, gram)


def final_call(place, own, other, inverse, tall):
    return pl.pallas_call(
        final_kernel,
        out_shape=(jax.ShapeDtypeStruct((K, D), jnp.float32), jax.ShapeDtypeStruct(tall.shape, jnp.float32)),
        in_specs=[SM, SM, SM, VM, VM, VM, VM],
        out_specs=(ANY, ANY),
        scratch_shapes=[
            pltpu.VMEM((K, D), jnp.float32),
            pltpu.VMEM(tall.shape, jnp.float32),
            pltpu.SemaphoreType.DMA((2,)),
        ],
        compiler_params=params(),
        name="final",
    )(*place, own, other, inverse, tall)


def on_device(data, sketch):
    place = [lax.axis_index(axis).astype(jnp.int32).reshape(1) for axis in ("core", "x", "y")]
    first, *parts = start_call(place, data, sketch)
    own, other, _ = sum_everywhere(parts[:2], parts[2:])
    inverse = factor_call(place[0], own)
    second, turned, gram, *give = middle_call(place, own, other, inverse, data)
    keep = keep_call(place, data, turned, gram)
    first_basis = exact_dot(first, ROOT_ROWS * inverse, ((1,), (1,)))
    own, other, first_basis = sum_everywhere(give, keep, first_basis)
    inverse = factor_call(place[0], own)
    projected, basis = final_call(place, own, other, inverse, second)
    return (first_basis, basis, projected)


def solution(mesh):
    split = Mesh(mesh.devices.reshape(Z, X, C, Y), AXES)
    return jax.shard_map(
        on_device,
        mesh=split,
        in_specs=(P(AXES, None), P()),
        out_specs=(P(AXES, None), P(AXES, None), P()),
        check_vma=False,
    )
```
